256 devices in a mesh: ctx: 16 (over y, x_lo, core), chan: 16 (over x_hi, z).
Axes of the slice: x: 4 (x_hi: 2, x_lo: 2; x = x_hi * 2 + x_lo), y: 4, z: 8, core: 2. Of those that a mesh axis runs over, the one named last changes fastest.
Arguments:
- features: bfloat16 [3, 12288, 8192], P(None, 'ctx', 'chan'), may hold values from -6 to 6
- pool_tails: bfloat16 [32, 3, 133, 8192], P('ctx', None, None, 'chan'), may hold values from -6 to 6
- short_filter: bfloat16 [7, 3, 8192], P(None, None, 'chan'), may hold values from -2 to 2
- long_filter: bfloat16 [512, 128], P('chan'), may hold values from -0.5 to 0.5
- skip_gain: float32 [8192], P('chan'), may hold values from -4 to 4
- out_weight: bfloat16 [8192, 8192], P('chan', 'ctx'), may hold values from -0.09375 to 0.09375
- stripe_request: int32 [16], replicated, may hold values from 0 to 3, never falling along the last dimension, each value on 1 to 8 neighbouring positions
- hit_holder: int32 [4], replicated, may hold values from 0 to 15
- hit_block: int32 [4], replicated, may hold values from 0 to 1
Outputs:
- mixed: bfloat16 [12288, 8192], P('ctx', 'chan')
The draws below stay inside these ranges and needn't reach their ends.
Inputs may be any that keep to these rules, and one draw needn't show every extreme that they name: `stripe_request`: request ids never fall along the stripes, and every request holds one or more stripes.
All inputs are finite; a program needn't handle non-finite values.
Results may differ from the reference program's by a relative error of at most 0.018.
Values may be sent and summed in bfloat16 or wider, within the bound.
No kernel may reach another device: no remote copies, remote signals or barrier semaphores. Data moves between devices by JAX's collectives and lax.ppermute only.
A program may use at most 128 MiB of HBM per device.

```python
import math
import jax
import jax.numpy as jnp
import numpy as np
from jax import lax

D = 8192
GROUP = 16
LONG = 128
SHORT = 7
TOK_DEV = 768
POOL_DEV = 2
REQS = 4
TOKENS = 12288
TAIL = 133
POOL = 32
GROUPS = 512
N_CTX = 16
N_CHAN = 16


def plant(values, stream_key, least, largest):
    longest = values.shape.index(max(values.shape))
    spots = []
    for shift in (0, 1):
        where = [jax.random.randint(jax.random.fold_in(stream_key, axis), (), 0, length) for axis, length in enumerate(values.shape)]
        where[longest] = (where[longest] + shift) % values.shape[longest]
        spots.append(tuple(where))
    return values.at[spots[0]].set(least).at[spots[1]].set(largest)


def strengthened(drawn, stream_key, source, target, parts, factor):
    owner, partner = [(jnp.arange(drawn.shape[dim]) // (drawn.shape[dim] // parts)).reshape([-1 if axis == dim else 1 for axis in range(drawn.ndim)]) for dim in (source, target)]
    chosen = jax.random.permutation(stream_key, parts)[partner]
    strong = (owner == chosen) | (owner == (partner + parts // 2) % parts)
    return jnp.where(strong, factor * drawn, drawn)


def levels(rng, extent, pieces, low, top_value):
    loudness, own = 1.0, jax.random.fold_in(rng, 6)
    for dim, shards_of in pieces:
        steps = jnp.exp(jax.random.uniform(jax.random.fold_in(own, dim), (shards_of,), jnp.float32, low / len(pieces), top_value / len(pieces)))
        loudness = loudness * jnp.repeat(steps, extent[dim] // shards_of).reshape([-1 if axis == dim else 1 for axis in range(len(extent))])
    return loudness


def profile(count, total, reach, slope):
    weights = [(1 << 20) // math.isqrt(grade ** slope) + 1 for grade in range(2, count + 1)]
    surplus, given = total - reach - (count - 1), [1] * (count - 1)
    while surplus > 0:
        free = [i for i in range(count - 1) if given[i] < reach]
        pool, budget = sum([weights[i] for i in free]), surplus
        for i in free:
            extra = min(reach - given[i], max(1, budget * weights[i] // pool), surplus)
            given[i] = given[i] + extra
            surplus = surplus - extra
    return np.array([reach] + given)


def ragged_sizes(own_key, number_of, total, limit, skew):
    if number_of == 2:
        one = jax.random.randint(own_key, (), max(1, total - limit), min(limit, total - 1) + 1)
        return jnp.stack([one, total - one])
    tallies = jnp.asarray(profile(number_of, total, limit, skew), jnp.int32)
    twos = (number_of - 1) // 2
    donor, taker = tallies[1:1 + 2 * twos:2], tallies[2:2 + 2 * twos:2]
    margin = jnp.minimum(donor - 1, limit - taker)
    moved = jax.random.randint(jax.random.fold_in(own_key, 1), (twos,), 0, 1 << 20) % (margin + 1)
    tallies = tallies.at[1:1 + 2 * twos:2].set(donor - moved).at[2:2 + 2 * twos:2].set(taker + moved)
    return tallies[jax.random.permutation(jax.random.fold_in(own_key, 2), number_of)]


def normal_values(own_key, extent, deviation, reach, split=(), held_as=jnp.bfloat16):
    result = deviation * jax.random.normal(own_key, extent, jnp.float32)
    if split:
        result = result * levels(own_key, extent, split, -0.22, 0.18)
    return jnp.clip(result, -reach, reach).astype(held_as)


def bell_draw_with(key, extent, deviation, bound, split, heavy, kind=jnp.bfloat16):
    drawn = deviation * jax.random.normal(key, extent, jnp.float32)
    if split:
        drawn = drawn * levels(key, extent, split, -0.22, 0.18)
    return jnp.clip(strengthened(drawn, jax.random.fold_in(key, 3), *heavy), -bound, bound).astype(kind)


def setup_inputs(seed: int = 0) -> dict:
    seeds = jax.random.split(jax.random.key(seed), 10)
    return {
        "features": normal_values(seeds[0], (3, TOKENS, D), 1.0, 6.0, ((1, 16), (2, 16))),
        "pool_tails": normal_values(seeds[1], (POOL, 3, TAIL, D), 1.0, 6.0, ((0, 16), (3, 16))),
        "short_filter": normal_values(seeds[2], (SHORT, 3, D), SHORT ** -0.5, 2.0, ((2, 16),)),
        "long_filter": normal_values(seeds[3], (GROUPS, LONG), LONG ** -0.5, 0.5, ((0, 16),)),
        "skip_gain": normal_values(seeds[4], (D,), 1.0, 4.0, ((0, 16),), jnp.float32),
        "out_weight": bell_draw_with(seeds[5], (D, D), D ** -0.5, 0.09375, ((0, 16), (1, 16)), (0, 1, 16, 2.0)),
        "stripe_request": jnp.searchsorted(jnp.cumsum(ragged_sizes(seeds[6], REQS, N_CTX, N_CTX // 2, 0)), jnp.arange(N_CTX), side="right").astype(jnp.int32),
        "hit_holder": plant(jax.random.randint(seeds[7], (REQS,), 0, N_CTX), jax.random.fold_in(seeds[7], 1), 0, N_CTX - 1).astype(jnp.int32),
        "hit_block": plant(jax.random.randint(seeds[8], (REQS,), 0, POOL_DEV), jax.random.fold_in(seeds[8], 1), 0, POOL_DEV - 1).astype(jnp.int32),
    }


def short_filtering(extended, taps):
    length = extended.shape[1] - SHORT + 1
    total = jnp.zeros((extended.shape[0], length, extended.shape[2]), jnp.float32)
    for offset in range(SHORT):
        begin = SHORT - 1 - offset
        total = total + taps[offset][:, None, :] * extended[:, begin:begin + length, :].astype(jnp.float32)
    return total


def reference(features, pool_tails, short_filter, long_filter, skip_gain, out_weight, stripe_request, hit_holder, hit_block):
    taps = short_filter.astype(jnp.float32)
    spread = jnp.repeat(long_filter.astype(jnp.float32), GROUP, axis=0)
    width = D // N_CHAN

    def one_stripe(stripe):
        stripe = stripe.astype(jnp.int32)
        request = stripe_request[stripe]
        earlier = stripe_request[jnp.maximum(stripe - 1, 0)]
        starting = jnp.logical_or(stripe == 0, earlier != request)
        slot = (hit_holder[request] * POOL_DEV + hit_block[request]).astype(jnp.int32)
        pooled = lax.dynamic_index_in_dim(pool_tails, slot, 0, keepdims=False)
        begin = jnp.maximum(stripe * TOK_DEV - TAIL, 0).astype(jnp.int32)
        previous = lax.dynamic_slice_in_dim(features, begin, TAIL, 1)
        rim = jnp.where(starting, pooled, previous)
        own = lax.dynamic_slice_in_dim(features, (stripe * TOK_DEV).astype(jnp.int32), TOK_DEV, 1)
        extended = jnp.concatenate([rim, own], axis=1)
        filtered = short_filtering(extended, taps)
        product = (filtered[1] * filtered[2]).astype(jnp.bfloat16)
        wide = product.astype(jnp.float32)

        def add_tap(lag, total):
            lag = lag.astype(jnp.int32)
            window = lax.dynamic_slice_in_dim(wide, (LONG - 1 - lag).astype(jnp.int32), TOK_DEV, 0)
            column = lax.dynamic_slice_in_dim(spread, lag, 1, 1)[:, 0]
            return total + column[None, :] * window

        long_out = lax.fori_loop(jnp.int32(0), jnp.int32(LONG), add_tap, jnp.zeros((TOK_DEV, D), jnp.float32))
        gated = (filtered[0, LONG - 1:] * (long_out + skip_gain[None, :] * wide[LONG - 1:])).astype(jnp.bfloat16)

        def add_part(block, total):
            start = (block.astype(jnp.int32) * width).astype(jnp.int32)
            rows = lax.dynamic_slice_in_dim(gated, start, width, 1)
            weights = lax.dynamic_slice_in_dim(out_weight, start, width, 0)
            part = jnp.dot(rows, weights, preferred_element_type=jnp.float32).astype(jnp.bfloat16)
            part = lax.optimization_barrier(part)
            return total + part.astype(jnp.float32)

        summed = lax.fori_loop(jnp.int32(0), jnp.int32(N_CHAN), add_part, jnp.zeros((TOK_DEV, D), jnp.float32))
        return summed.astype(jnp.bfloat16)

    blocks = lax.map(one_stripe, jnp.arange(N_CTX, dtype=jnp.int32))
    return blocks.reshape(N_CTX * TOK_DEV, D)
```

```python
import jax
import jax.numpy as jnp
from jax import lax
from jax.experimental import pallas as pl
from jax.experimental.pallas import tpu as pltpu
from jax.sharding import PartitionSpec as P

LANES = 128
HEAD = 144
F32 = jnp.float32
BF16 = jnp.bfloat16


def toeplitz_kernel(rows_ref, out_ref):
    long_len, width = LANES, rows_ref.shape[1]
    for g in range(rows_ref.shape[0]):
        wide = jnp.broadcast_to(rows_ref[g : g + 1, :], (long_len, width))
        band = pltpu.roll(wide, 0, 1, stride=1, stride_axis=0)
        out_ref[g * long_len : (g + 1) * long_len, :] = band.astype(BF16)


def toeplitz(long_filter):
    groups, long_len = long_filter.shape
    rows = jnp.pad(long_filter[:, ::-1].astype(F32), ((0, 0), (1, long_len - 1)))
    return pl.pallas_call(
        toeplitz_kernel,
        grid=(groups // 8,),
        in_specs=[pl.BlockSpec((8, 2 * long_len), lambda i: (i, 0))],
        out_specs=pl.BlockSpec((8 * long_len, 2 * long_len), lambda i: (i, 0)),
        out_shape=jax.ShapeDtypeStruct((groups * long_len, 2 * long_len), BF16),
        name="toeplitz",
    )(rows)


def conv_kernel(head_ref, body_ref, taps_ref, skip_ref, band_ref, out_ref, ext, prod):
    short_len = taps_ref.shape[1]
    tokens = body_ref.shape[1]
    blocks = tokens // LANES
    ext[:, :HEAD, :] = head_ref[...].astype(F32)
    ext[:, HEAD:, :] = body_ref[...].astype(F32)

    def short(s, begin):
        total = None
        for j in range(short_len):
            term = taps_ref[s, j : j + 1, :] * ext[s, begin + 16 - j : begin + 16 - j + LANES, :]
            total = term if total is None else total + term
        return total

    for n in range(blocks + 1):
        prod[n * LANES : (n + 1) * LANES, :] = (
            short(1, n * LANES) * short(2, n * LANES)
        ).astype(BF16)
    group = lax.broadcasted_iota(jnp.int32, (LANES, LANES), 1) // 16
    for n in range(blocks):
        window = prod[n * LANES : (n + 2) * LANES, :]
        every = jnp.dot(band_ref[...], window, preferred_element_type=F32)
        long_out = every[:LANES]
        for g in range(1, 8):
            long_out = jnp.where(group == g, every[g * LANES : (g + 1) * LANES], long_out)
        direct = prod[(n + 1) * LANES : (n + 2) * LANES, :].astype(F32)
        query = short(0, (n + 1) * LANES)
        out_ref[n * LANES : (n + 1) * LANES, :] = (
            query * (long_out + skip_ref[...] * direct)
        ).astype(BF16)


def gated_tokens(head, body, taps, skip, band):
    sets, tokens, channels = body.shape
    return pl.pallas_call(
        conv_kernel,
        grid=(channels // LANES,),
        in_specs=[
            pl.BlockSpec((sets, HEAD, LANES), lambda i: (0, 0, i)),
            pl.BlockSpec((sets, tokens, LANES), lambda i: (0, 0, i)),
            pl.BlockSpec((sets, taps.shape[1], LANES), lambda i: (0, 0, i)),
            pl.BlockSpec((1, LANES), lambda i: (0, i)),
            pl.BlockSpec((8 * LANES, 2 * LANES), lambda i: (i, 0)),
        ],
        out_specs=pl.BlockSpec((tokens, LANES), lambda i: (0, i)),
        out_shape=jax.ShapeDtypeStruct((tokens, channels), BF16),
        scratch_shapes=[
            pltpu.VMEM((sets, HEAD + tokens, LANES), F32),
            pltpu.VMEM((LANES + tokens, LANES), BF16),
        ],
        compiler_params=pltpu.CompilerParams(vmem_limit_bytes=48 * 1024 * 1024),
        name="conv",
    )(head, body, taps, skip, band)


def project_kernel(gated_ref, weights_ref, out_ref):
    total = None
    for k in range(gated_ref.shape[0]):
        term = jnp.dot(gated_ref[k], weights_ref[0, k, 0], preferred_element_type=F32)
        total = term if total is None else total + term
    out_ref[0] = total.astype(BF16)


def project(gated, weights):
    parts, tokens, depth = gated.shape
    width = weights.shape[-1]
    return pl.pallas_call(
        project_kernel,
        grid=(4,),
        in_specs=[
            pl.BlockSpec((parts, tokens, depth), lambda s: (0, 0, 0)),
            pl.BlockSpec((1, parts, 1, depth, width), lambda s: (s // 2, 0, s % 2, 0, 0)),
        ],
        out_specs=pl.BlockSpec((1, tokens, width), lambda s: (s, 0, 0)),
        out_shape=jax.ShapeDtypeStruct((4, tokens, width), BF16),
        compiler_params=pltpu.CompilerParams(vmem_limit_bytes=48 * 1024 * 1024),
        name="project",
    )(gated, weights)


def swapped_pairs():
    pairs = []
    for ctx in range(16):
        for chan in range(16):
            inner, ring = (ctx >> 1) & 3, (chan >> 1) & 3
            to_ctx = (ctx & 9) | (ring << 1)
            to_chan = (chan & 9) | (inner << 1)
            pairs.append((ctx * 16 + chan, to_ctx * 16 + to_chan))
    return pairs


def grouped(value, groups):
    return lax.all_to_all(
        value, "chan", split_axis=0, concat_axis=0, tiled=True, axis_index_groups=groups
    )


def pool_pieces(pool_tails):
    pool_dev, sets, tail, channels = pool_tails.shape
    rows = jnp.transpose(pool_tails, (1, 2, 0, 3)).reshape(sets * tail, pool_dev, channels)
    count = lax.axis_size("ctx")
    each = -(-(sets * tail) // count)
    rows = jnp.pad(rows, ((0, each * count - sets * tail), (0, 0), (0, 0)))
    return rows.reshape(count, each, pool_dev, channels)


def chosen_pieces(pieces, stripe_request, hit_holder, hit_block):
    count, _, pool_dev, _ = pieces.shape
    request = jnp.arange(hit_holder.shape[0], dtype=jnp.int32)
    ours = (stripe_request[:, None] == request[None, :]).astype(jnp.int32)
    holder = jnp.sum(ours * hit_holder[None, :], axis=1)
    block = jnp.sum(ours * hit_block[None, :], axis=1)
    select = jnp.logical_and(
        holder[:, None, None] == jnp.arange(count, dtype=jnp.int32)[None, :, None],
        block[:, None, None] == jnp.arange(pool_dev, dtype=jnp.int32)[None, None, :],
    ).astype(BF16)
    return jnp.einsum("dhb,hrbc->drc", select, pieces, preferred_element_type=F32).astype(BF16)


def exchanged(value):
    return lax.all_to_all(value, "ctx", split_axis=0, concat_axis=0, tiled=True)


def body(
    features,
    pool_tails,
    short_filter,
    long_filter,
    skip_gain,
    out_weight,
    stripe_request,
    hit_holder,
    hit_block,
):
    sets, tokens, channels = features.shape
    tail = pool_tails.shape[2]
    split = 2 * LANES
    my_index = lax.axis_index("ctx")
    rings = [[j | (r << 1) for r in range(4)] for j in (0, 1, 8, 9)]
    pairs = [[j | (r << 1) for j in (0, 1, 8, 9)] for r in range(4)]

    def spread(gated):
        return grouped(jnp.broadcast_to(gated, (4, *gated.shape)), rings)

    pieces = exchanged(pool_pieces(pool_tails))
    swapped = lax.ppermute(out_weight, ("ctx", "chan"), swapped_pairs())
    taps = jnp.transpose(short_filter, (1, 0, 2)).astype(F32)
    skip = skip_gain[None, :]
    band = toeplitz(long_filter)
    late = gated_tokens(
        features[:, split - HEAD : split, :], features[:, split:, :], taps, skip, band
    )
    previous = lax.ppermute(
        features[:, tokens - HEAD :, :], "ctx", [(i, i + 1) for i in range(15)]
    )
    pulled = exchanged(chosen_pieces(pieces, stripe_request, hit_holder, hit_block))
    swapped, pulled, late = lax.optimization_barrier((swapped, pulled, late))
    weights = lax.all_gather(swapped, "ctx", axis=0, tiled=True)
    weights = weights.reshape(2, 4, 2, *out_weight.shape)
    late = spread(late)
    pulled = pulled.reshape(-1, channels)[: sets * tail].reshape(sets, tail, channels)

    order = jnp.arange(stripe_request.shape[0], dtype=jnp.int32)
    request = jnp.sum(jnp.where(order == my_index, stripe_request, 0))
    earlier = jnp.sum(jnp.where(order == my_index - 1, stripe_request, 0))
    starting = jnp.logical_or(my_index == 0, earlier != request)
    pulled = jnp.pad(pulled, ((0, 0), (HEAD - tail, 0), (0, 0)))
    head = jnp.where(starting, pulled, previous)
    early = gated_tokens(head, features[:, :split, :], taps, skip, band)
    early, late = lax.optimization_barrier((early, late))
    early, partial = lax.optimization_barrier((spread(early), project(late, weights)))
    late = grouped(partial, pairs)
    early, late = lax.optimization_barrier((project(early, weights), late))
    early = grouped(early, pairs)

    def mixed(arrived):
        return jnp.sum(arrived.astype(F32), axis=0).astype(BF16)

    return jnp.concatenate([mixed(early), mixed(late)], axis=0)


def solution(mesh):
    return jax.shard_map(
        body,
        mesh=mesh,
        in_specs=(
            P(None, "ctx", "chan"),
            P("ctx", None, None, "chan"),
            P(None, None, "chan"),
            P("chan", None),
            P("chan"),
            P("chan", "ctx"),
            P(),
            P(),
            P(),
        ),
        out_specs=P("ctx", "chan"),
        check_vma=False,
    )
```

```python
import jax
import jax.numpy as jnp
from jax import lax
from jax.experimental import pallas as pl
from jax.experimental.pallas import tpu as pltpu
from jax.sharding import PartitionSpec as P

LANES = 128
HEAD = 144
F32 = jnp.float32
BF16 = jnp.bfloat16


def toeplitz_kernel(rows_ref, out_ref):
    long_len, width = LANES, rows_ref.shape[1]
    for g in range(rows_ref.shape[0]):
        wide = jnp.broadcast_to(rows_ref[g : g + 1, :], (long_len, width))
        band = pltpu.roll(wide, 0, 1, stride=1, stride_axis=0)
        out_ref[g * long_len : (g + 1) * long_len, :] = band.astype(BF16)


def toeplitz(long_filter):
    groups, long_len = long_filter.shape
    rows = jnp.pad(long_filter[:, ::-1].astype(F32), ((0, 0), (1, long_len - 1)))
    return pl.pallas_call(
        toeplitz_kernel,
        grid=(groups // 8,),
        in_specs=[pl.BlockSpec((8, 2 * long_len), lambda i: (i, 0))],
        out_specs=pl.BlockSpec((8 * long_len, 2 * long_len), lambda i: (i, 0)),
        out_shape=jax.ShapeDtypeStruct((groups * long_len, 2 * long_len), BF16),
        name="toeplitz",
    )(rows)


def conv_kernel(head_ref, body_ref, taps_ref, skip_ref, band_ref, out_ref, ext, prod):
    short_len = taps_ref.shape[1]
    tokens = body_ref.shape[1]
    blocks = tokens // LANES
    ext[:, :HEAD, :] = head_ref[...].astype(F32)
    ext[:, HEAD:, :] = body_ref[...].astype(F32)

    def short(s, begin):
        total = None
        for j in range(short_len):
            term = taps_ref[s, j : j + 1, :] * ext[s, begin + 16 - j : begin + 16 - j + LANES, :]
            total = term if total is None else total + term
        return total

    for n in range(blocks + 1):
        prod[n * LANES : (n + 1) * LANES, :] = (
            short(1, n * LANES) * short(2, n * LANES)
        ).astype(BF16)
    group = lax.broadcasted_iota(jnp.int32, (LANES, LANES), 1) // 16
    for n in range(blocks):
        window = prod[n * LANES : (n + 2) * LANES, :]
        every = jnp.dot(band_ref[...], window, preferred_element_type=F32)
        long_out = every[:LANES]
        for g in range(1, 8):
            long_out = jnp.where(group == g, every[g * LANES : (g + 1) * LANES], long_out)
        direct = prod[(n + 1) * LANES : (n + 2) * LANES, :].astype(F32)
        query = short(0, (n + 1) * LANES)
        out_ref[n * LANES : (n + 1) * LANES, :] = (
            query * (long_out + skip_ref[...] * direct)
        ).astype(BF16)


def gated_tokens(head, body, taps, skip, band):
    sets, tokens, channels = body.shape
    return pl.pallas_call(
        conv_kernel,
        grid=(channels // LANES,),
        in_specs=[
            pl.BlockSpec((sets, HEAD, LANES), lambda i: (0, 0, i)),
            pl.BlockSpec((sets, tokens, LANES), lambda i: (0, 0, i)),
            pl.BlockSpec((sets, taps.shape[1], LANES), lambda i: (0, 0, i)),
            pl.BlockSpec((1, LANES), lambda i: (0, i)),
            pl.BlockSpec((8 * LANES, 2 * LANES), lambda i: (i, 0)),
        ],
        out_specs=pl.BlockSpec((tokens, LANES), lambda i: (0, i)),
        out_shape=jax.ShapeDtypeStruct((tokens, channels), BF16),
        scratch_shapes=[
            pltpu.VMEM((sets, HEAD + tokens, LANES), F32),
            pltpu.VMEM((LANES + tokens, LANES), BF16),
        ],
        compiler_params=pltpu.CompilerParams(vmem_limit_bytes=48 * 1024 * 1024),
        name="conv",
    )(head, body, taps, skip, band)


def project_kernel(side_ref, *refs):
    weights_ref, out_ref = refs[-2:]
    begin = 0
    for gated_ref in refs[:-2]:
        total = None
        for k in range(gated_ref.shape[0]):
            term = jnp.dot(gated_ref[k], weights_ref[0, k, 0], preferred_element_type=F32)
            total = term if total is None else total + term
        out_ref[0, begin : begin + gated_ref.shape[1], :] = total.astype(BF16)
        begin += gated_ref.shape[1]


def project(runs, weights, side):
    parts, _, depth = runs[0].shape
    tokens = sum(run.shape[1] for run in runs)
    width = weights.shape[-1]
    return pl.pallas_call(
        project_kernel,
        grid_spec=pltpu.PrefetchScalarGridSpec(
            num_scalar_prefetch=1,
            grid=(2,),
            in_specs=[pl.BlockSpec(run.shape, lambda s, side: (0, 0, 0)) for run in runs]
            + [pl.BlockSpec((1, parts, 1, depth, width), lambda s, side: (side[0], 0, s, 0, 0))],
            out_specs=pl.BlockSpec((1, tokens, width), lambda s, side: (s, 0, 0)),
        ),
        out_shape=jax.ShapeDtypeStruct((2, tokens, width), BF16),
        compiler_params=pltpu.CompilerParams(vmem_limit_bytes=48 * 1024 * 1024),
        name="project",
    )(jnp.reshape(side, (1,)).astype(jnp.int32), *runs, weights)


def swapped_pairs():
    pairs = []
    for ctx in range(16):
        for chan in range(16):
            inner, ring = (ctx >> 1) & 3, (chan >> 1) & 3
            to_ctx = (ctx & 9) | (ring << 1)
            to_chan = (chan & 9) | (inner << 1)
            pairs.append((ctx * 16 + chan, to_ctx * 16 + to_chan))
    return pairs


def grouped(value, groups):
    return lax.all_to_all(
        value, "chan", split_axis=0, concat_axis=0, tiled=True, axis_index_groups=groups
    )


def pool_pieces(pool_tails):
    pool_dev, sets, tail, channels = pool_tails.shape
    rows = jnp.transpose(pool_tails, (1, 2, 0, 3)).reshape(sets * tail, pool_dev, channels)
    count = lax.axis_size("ctx")
    each = -(-(sets * tail) // count)
    rows = jnp.pad(rows, ((0, each * count - sets * tail), (0, 0), (0, 0)))
    return rows.reshape(count, each, pool_dev, channels)


def chosen_pieces(pieces, stripe_request, hit_holder, hit_block):
    count, _, pool_dev, _ = pieces.shape
    request = jnp.arange(hit_holder.shape[0], dtype=jnp.int32)
    ours = (stripe_request[:, None] == request[None, :]).astype(jnp.int32)
    holder = jnp.sum(ours * hit_holder[None, :], axis=1)
    block = jnp.sum(ours * hit_block[None, :], axis=1)
    select = jnp.logical_and(
        holder[:, None, None] == jnp.arange(count, dtype=jnp.int32)[None, :, None],
        block[:, None, None] == jnp.arange(pool_dev, dtype=jnp.int32)[None, None, :],
    ).astype(BF16)
    return jnp.einsum("dhb,hrbc->drc", select, pieces, preferred_element_type=F32).astype(BF16)


def exchanged(value):
    return lax.all_to_all(value, "ctx", split_axis=0, concat_axis=0, tiled=True)


def body(
    features,
    pool_tails,
    short_filter,
    long_filter,
    skip_gain,
    out_weight,
    stripe_request,
    hit_holder,
    hit_block,
):
    sets, tokens, channels = features.shape
    tail = pool_tails.shape[2]
    split = 2 * LANES
    my_index = lax.axis_index("ctx")
    rings = [[j | (r << 1) for r in range(4)] for j in (0, 1, 8, 9)]

    def spread(gated):
        return grouped(jnp.broadcast_to(gated, (4, *gated.shape)), rings)

    pieces = exchanged(pool_pieces(pool_tails))
    swapped = lax.ppermute(out_weight, ("ctx", "chan"), swapped_pairs())
    taps = jnp.transpose(short_filter, (1, 0, 2)).astype(F32)
    skip = skip_gain[None, :]
    band = toeplitz(long_filter)
    late = gated_tokens(
        features[:, split - HEAD : split, :], features[:, split:, :], taps, skip, band
    )
    previous = lax.ppermute(
        features[:, tokens - HEAD :, :], "ctx", [(i, i + 1) for i in range(15)]
    )
    pulled = exchanged(chosen_pieces(pieces, stripe_request, hit_holder, hit_block))
    swapped, pulled, late = lax.optimization_barrier((swapped, pulled, late))
    weights = lax.all_gather(swapped, "ctx", axis=0, tiled=True)
    weights = weights.reshape(2, 4, 2, *out_weight.shape)
    late = spread(late)
    pulled = pulled.reshape(-1, channels)[: sets * tail].reshape(sets, tail, channels)

    order = jnp.arange(stripe_request.shape[0], dtype=jnp.int32)
    request = jnp.sum(jnp.where(order == my_index, stripe_request, 0))
    earlier = jnp.sum(jnp.where(order == my_index - 1, stripe_request, 0))
    starting = jnp.logical_or(my_index == 0, earlier != request)
    pulled = jnp.pad(pulled, ((0, 0), (HEAD - tail, 0), (0, 0)))
    head = jnp.where(starting, pulled, previous)
    early = gated_tokens(head, features[:, :split, :], taps, skip, band)
    early, late = lax.optimization_barrier((early, late))
    early, late = [spread(early)], [late]

    chan = lax.axis_index("chan")
    high, low = chan >> 3, chan & 1

    def flipped(value, bit):
        return lax.ppermute(value, "chan", [(j, j ^ bit) for j in range(16)])

    def halves(kept, came):
        kept = kept.astype(F32) + came.astype(F32)
        mine = jnp.where(low == 0, kept[0], kept[1])
        other = jnp.where(low == 0, kept[1], kept[0])
        return mine, other.astype(BF16)

    def rounded(mine, came):
        return (mine + came.astype(F32)).astype(BF16)

    late_came = flipped(project(late, weights, 1 - high), 8)
    late_kept = project(late, weights, high)
    early, late_kept = lax.optimization_barrier((early, late_kept))
    early_came = flipped(project(early, weights, 1 - high), 8)
    late_mine, late_other = halves(late_kept, late_came)
    early, late_other = lax.optimization_barrier((early, late_other))
    late_came = flipped(late_other, 1)
    early_mine, early_other = halves(project(early, weights, high), early_came)
    early_came = flipped(early_other, 1)
    return jnp.concatenate(
        [rounded(early_mine, early_came), rounded(late_mine, late_came)], axis=0
    )


def solution(mesh):
    return jax.shard_map(
        body,
        mesh=mesh,
        in_specs=(
            P(None, "ctx", "chan"),
            P("ctx", None, None, "chan"),
            P(None, None, "chan"),
            P("chan", None),
            P("chan"),
            P("chan", "ctx"),
            P(),
            P(),
            P(),
        ),
        out_specs=P("ctx", "chan"),
        check_vma=False,
    )
```

```python
import jax
import jax.numpy as jnp
from jax import lax
from jax.experimental import pallas as pl
from jax.experimental.pallas import tpu as pltpu
from jax.sharding import PartitionSpec as P

LANES = 128
HEAD = 144
F32 = jnp.float32
BF16 = jnp.bfloat16


def toeplitz_kernel(rows_ref, out_ref):
    long_len, width = LANES, rows_ref.shape[1]
    for g in range(rows_ref.shape[0]):
        wide = jnp.broadcast_to(rows_ref[g : g + 1, :], (long_len, width))
        band = pltpu.roll(wide, 0, 1, stride=1, stride_axis=0)
        out_ref[g * long_len : (g + 1) * long_len, :] = band.astype(BF16)


def toeplitz(long_filter):
    groups, long_len = long_filter.shape
    rows = jnp.pad(long_filter[:, ::-1].astype(F32), ((0, 0), (1, long_len - 1)))
    return pl.pallas_call(
        toeplitz_kernel,
        grid=(groups // 8,),
        in_specs=[pl.BlockSpec((8, 2 * long_len), lambda i: (i, 0))],
        out_specs=pl.BlockSpec((8 * long_len, 2 * long_len), lambda i: (i, 0)),
        out_shape=jax.ShapeDtypeStruct((groups * long_len, 2 * long_len), BF16),
        name="toeplitz",
    )(rows)


def conv_kernel(head_ref, body_ref, taps_ref, skip_ref, band_ref, out_ref, ext, prod):
    short_len = taps_ref.shape[1]
    tokens = body_ref.shape[1]
    blocks = tokens // LANES
    ext[:, :HEAD, :] = head_ref[...].astype(F32)
    ext[:, HEAD:, :] = body_ref[...].astype(F32)

    def short(s, begin):
        total = None
        for j in range(short_len):
            term = taps_ref[s, j : j + 1, :] * ext[s, begin + 16 - j : begin + 16 - j + LANES, :]
            total = term if total is None else total + term
        return total

    for n in range(blocks + 1):
        prod[n * LANES : (n + 1) * LANES, :] = (
            short(1, n * LANES) * short(2, n * LANES)
        ).astype(BF16)
    group = lax.broadcasted_iota(jnp.int32, (LANES, LANES), 1) // 16
    for n in range(blocks):
        window = prod[n * LANES : (n + 2) * LANES, :]
        every = jnp.dot(band_ref[...], window, preferred_element_type=F32)
        long_out = every[:LANES]
        for g in range(1, 8):
            long_out = jnp.where(group == g, every[g * LANES : (g + 1) * LANES], long_out)
        direct = prod[(n + 1) * LANES : (n + 2) * LANES, :].astype(F32)
        query = short(0, (n + 1) * LANES)
        out_ref[n * LANES : (n + 1) * LANES, :] = (
            query * (long_out + skip_ref[...] * direct)
        ).astype(BF16)


def gated_tokens(head, body, taps, skip, band):
    sets, tokens, channels = body.shape
    return pl.pallas_call(
        conv_kernel,
        grid=(channels // LANES,),
        in_specs=[
            pl.BlockSpec((sets, HEAD, LANES), lambda i: (0, 0, i)),
            pl.BlockSpec((sets, tokens, LANES), lambda i: (0, 0, i)),
            pl.BlockSpec((sets, taps.shape[1], LANES), lambda i: (0, 0, i)),
            pl.BlockSpec((1, LANES), lambda i: (0, i)),
            pl.BlockSpec((8 * LANES, 2 * LANES), lambda i: (i, 0)),
        ],
        out_specs=pl.BlockSpec((tokens, LANES), lambda i: (0, i)),
        out_shape=jax.ShapeDtypeStruct((tokens, channels), BF16),
        scratch_shapes=[
            pltpu.VMEM((sets, HEAD + tokens, LANES), F32),
            pltpu.VMEM((LANES + tokens, LANES), BF16),
        ],
        compiler_params=pltpu.CompilerParams(vmem_limit_bytes=48 * 1024 * 1024),
        name="conv",
    )(head, body, taps, skip, band)


def project_kernel(side_ref, *refs):
    weights_ref, out_ref = refs[-2:]
    begin = 0
    for gated_ref in refs[:-2]:
        total = None
        for k in range(gated_ref.shape[0]):
            term = jnp.dot(gated_ref[k], weights_ref[0, k, 0], preferred_element_type=F32)
            total = term if total is None else total + term
        out_ref[0, begin : begin + gated_ref.shape[1], :] = total.astype(BF16)
        begin += gated_ref.shape[1]


def project(runs, weights, side, dim):
    parts, _, depth = runs[0].shape
    tokens = sum(run.shape[1] for run in runs)
    width = weights.shape[-1]

    def block(s, side):
        return (side[0], 0, s, 0, 0) if dim == 0 else (s, 0, side[0], 0, 0)

    return pl.pallas_call(
        project_kernel,
        grid_spec=pltpu.PrefetchScalarGridSpec(
            num_scalar_prefetch=1,
            grid=(2,),
            in_specs=[pl.BlockSpec(run.shape, lambda s, side: (0, 0, 0)) for run in runs]
            + [pl.BlockSpec((1, parts, 1, depth, width), block)],
            out_specs=pl.BlockSpec((1, tokens, width), lambda s, side: (s, 0, 0)),
        ),
        out_shape=jax.ShapeDtypeStruct((2, tokens, width), BF16),
        compiler_params=pltpu.CompilerParams(vmem_limit_bytes=48 * 1024 * 1024),
        name="project",
    )(jnp.reshape(side, (1,)).astype(jnp.int32), *runs, weights)


def swapped_pairs():
    pairs = []
    for ctx in range(16):
        for chan in range(16):
            inner, ring = (ctx >> 1) & 3, (chan >> 1) & 3
            to_ctx = (ctx & 9) | (ring << 1)
            to_chan = (chan & 9) | (inner << 1)
            pairs.append((ctx * 16 + chan, to_ctx * 16 + to_chan))
    return pairs


def grouped(value, groups):
    return lax.all_to_all(
        value, "chan", split_axis=0, concat_axis=0, tiled=True, axis_index_groups=groups
    )


def pool_pieces(pool_tails):
    pool_dev, sets, tail, channels = pool_tails.shape
    rows = jnp.transpose(pool_tails, (1, 2, 0, 3)).reshape(sets * tail, pool_dev, channels)
    count = lax.axis_size("ctx")
    each = -(-(sets * tail) // count)
    rows = jnp.pad(rows, ((0, each * count - sets * tail), (0, 0), (0, 0)))
    return rows.reshape(count, each, pool_dev, channels)


def chosen_pieces(pieces, stripe_request, hit_holder, hit_block):
    count, _, pool_dev, _ = pieces.shape
    request = jnp.arange(hit_holder.shape[0], dtype=jnp.int32)
    ours = (stripe_request[:, None] == request[None, :]).astype(jnp.int32)
    holder = jnp.sum(ours * hit_holder[None, :], axis=1)
    block = jnp.sum(ours * hit_block[None, :], axis=1)
    select = jnp.logical_and(
        holder[:, None, None] == jnp.arange(count, dtype=jnp.int32)[None, :, None],
        block[:, None, None] == jnp.arange(pool_dev, dtype=jnp.int32)[None, None, :],
    ).astype(BF16)
    return jnp.einsum("dhb,hrbc->drc", select, pieces, preferred_element_type=F32).astype(BF16)


def exchanged(value):
    return lax.all_to_all(value, "ctx", split_axis=0, concat_axis=0, tiled=True)


def body(
    features,
    pool_tails,
    short_filter,
    long_filter,
    skip_gain,
    out_weight,
    stripe_request,
    hit_holder,
    hit_block,
):
    sets, tokens, channels = features.shape
    tail = pool_tails.shape[2]
    split = 2 * LANES
    my_index = lax.axis_index("ctx")
    rings = [[j | (r << 1) for r in range(4)] for j in (0, 1, 8, 9)]

    def spread(gated):
        return grouped(jnp.broadcast_to(gated, (4, *gated.shape)), rings)

    pieces = exchanged(pool_pieces(pool_tails))
    swapped = lax.ppermute(out_weight, ("ctx", "chan"), swapped_pairs())
    taps = jnp.transpose(short_filter, (1, 0, 2)).astype(F32)
    skip = skip_gain[None, :]
    band = toeplitz(long_filter)
    late = gated_tokens(
        features[:, split - HEAD : split, :], features[:, split:, :], taps, skip, band
    )
    previous = lax.ppermute(
        features[:, tokens - HEAD :, :], "ctx", [(i, i + 1) for i in range(15)]
    )
    pulled = exchanged(chosen_pieces(pieces, stripe_request, hit_holder, hit_block))
    swapped, pulled, late = lax.optimization_barrier((swapped, pulled, late))
    weights = lax.all_gather(swapped, "ctx", axis=0, tiled=True)
    weights = weights.reshape(2, 4, 2, *out_weight.shape)
    late = spread(late)
    pulled = pulled.reshape(-1, channels)[: sets * tail].reshape(sets, tail, channels)

    order = jnp.arange(stripe_request.shape[0], dtype=jnp.int32)
    request = jnp.sum(jnp.where(order == my_index, stripe_request, 0))
    earlier = jnp.sum(jnp.where(order == my_index - 1, stripe_request, 0))
    starting = jnp.logical_or(my_index == 0, earlier != request)
    pulled = jnp.pad(pulled, ((0, 0), (HEAD - tail, 0), (0, 0)))
    head = jnp.where(starting, pulled, previous)
    early = gated_tokens(head, features[:, :split, :], taps, skip, band)
    early, late = lax.optimization_barrier((early, late))
    early, late = [spread(early)], [late]

    chan = lax.axis_index("chan")
    high, low = chan >> 3, chan & 1

    def flipped(value, bit):
        return lax.ppermute(value, "chan", [(j, j ^ bit) for j in range(16)])

    def halves(kept, came, place):
        kept = kept.astype(F32) + came.astype(F32)
        mine = jnp.where(place == 0, kept[0], kept[1])
        other = jnp.where(place == 0, kept[1], kept[0])
        return mine, other.astype(BF16)

    def rounded(mine, came):
        return (mine + came.astype(F32)).astype(BF16)

    late_came = flipped(project(late, weights, 1 - high, 0), 8)
    late_kept = project(late, weights, high, 0)
    early, late_kept = lax.optimization_barrier((early, late_kept))
    early_came = flipped(project(early, weights, 1 - low, 2), 1)
    late_mine, late_other = halves(late_kept, late_came, low)
    early, late_other = lax.optimization_barrier((early, late_other))
    late_came = flipped(late_other, 1)
    early_mine, early_other = halves(project(early, weights, low, 2), early_came, high)
    early_came = flipped(early_other, 8)
    return jnp.concatenate(
        [rounded(early_mine, early_came), rounded(late_mine, late_came)], axis=0
    )


def solution(mesh):
    return jax.shard_map(
        body,
        mesh=mesh,
        in_specs=(
            P(None, "ctx", "chan"),
            P("ctx", None, None, "chan"),
            P(None, None, "chan"),
            P("chan", None),
            P("chan"),
            P("chan", "ctx"),
            P(),
            P(),
            P(),
        ),
        out_specs=P("ctx", "chan"),
        check_vma=False,
    )
```

```python
import jax
import jax.numpy as jnp
from jax import lax
from jax.experimental import pallas as pl
from jax.experimental.pallas import tpu as pltpu
from jax.sharding import PartitionSpec as P

LANES = 128
HEAD = 144
F32 = jnp.float32
BF16 = jnp.bfloat16


def toeplitz_kernel(rows_ref, out_ref):
    long_len, width = LANES, rows_ref.shape[1]
    for g in range(rows_ref.shape[0]):
        wide = jnp.broadcast_to(rows_ref[g : g + 1, :], (long_len, width))
        band = pltpu.roll(wide, 0, 1, stride=1, stride_axis=0)
        out_ref[g * long_len : (g + 1) * long_len, :] = band.astype(BF16)


def toeplitz(long_filter):
    groups, long_len = long_filter.shape
    rows = jnp.pad(long_filter[:, ::-1].astype(F32), ((0, 0), (1, long_len - 1)))
    return pl.pallas_call(
        toeplitz_kernel,
        grid=(groups // 8,),
        in_specs=[pl.BlockSpec((8, 2 * long_len), lambda i: (i, 0))],
        out_specs=pl.BlockSpec((8 * long_len, 2 * long_len), lambda i: (i, 0)),
        out_shape=jax.ShapeDtypeStruct((groups * long_len, 2 * long_len), BF16),
        name="toeplitz",
    )(rows)


def conv_kernel(head_ref, body_ref, taps_ref, skip_ref, band_ref, out_ref, ext, prod):
    short_len = taps_ref.shape[1]
    tokens = body_ref.shape[1]
    blocks = tokens // LANES
    ext[:, :HEAD, :] = head_ref[...].astype(F32)
    ext[:, HEAD:, :] = body_ref[...].astype(F32)

    def short(s, begin):
        total = None
        for j in range(short_len):
            term = taps_ref[s, j : j + 1, :] * ext[s, begin + 16 - j : begin + 16 - j + LANES, :]
            total = term if total is None else total + term
        return total

    for n in range(blocks + 1):
        prod[n * LANES : (n + 1) * LANES, :] = (
            short(1, n * LANES) * short(2, n * LANES)
        ).astype(BF16)
    group = lax.broadcasted_iota(jnp.int32, (LANES, LANES), 1) // 16
    for n in range(blocks):
        window = prod[n * LANES : (n + 2) * LANES, :]
        every = jnp.dot(band_ref[...], window, preferred_element_type=F32)
        long_out = every[:LANES]
        for g in range(1, 8):
            long_out = jnp.where(group == g, every[g * LANES : (g + 1) * LANES], long_out)
        direct = prod[(n + 1) * LANES : (n + 2) * LANES, :].astype(F32)
        query = short(0, (n + 1) * LANES)
        out_ref[n * LANES : (n + 1) * LANES, :] = (
            query * (long_out + skip_ref[...] * direct)
        ).astype(BF16)


def gated_tokens(head, body, taps, skip, band):
    sets, tokens, channels = body.shape
    return pl.pallas_call(
        conv_kernel,
        grid=(channels // LANES,),
        in_specs=[
            pl.BlockSpec((sets, HEAD, LANES), lambda i: (0, 0, i)),
            pl.BlockSpec((sets, tokens, LANES), lambda i: (0, 0, i)),
            pl.BlockSpec((sets, taps.shape[1], LANES), lambda i: (0, 0, i)),
            pl.BlockSpec((1, LANES), lambda i: (0, i)),
            pl.BlockSpec((8 * LANES, 2 * LANES), lambda i: (i, 0)),
        ],
        out_specs=pl.BlockSpec((tokens, LANES), lambda i: (0, i)),
        out_shape=jax.ShapeDtypeStruct((tokens, channels), BF16),
        scratch_shapes=[
            pltpu.VMEM((sets, HEAD + tokens, LANES), F32),
            pltpu.VMEM((LANES + tokens, LANES), BF16),
        ],
        compiler_params=pltpu.CompilerParams(vmem_limit_bytes=48 * 1024 * 1024),
        name="conv",
    )(head, body, taps, skip, band)


def project_kernel(side_ref, *refs):
    weights_ref, out_ref = refs[-2:]
    begin = 0
    for gated_ref in refs[:-2]:
        total = None
        for k in range(gated_ref.shape[0]):
            term = jnp.dot(gated_ref[k], weights_ref[0, k, 0], preferred_element_type=F32)
            total = term if total is None else total + term
        out_ref[0, begin : begin + gated_ref.shape[1], :] = total.astype(BF16)
        begin += gated_ref.shape[1]


def project(runs, weights, side):
    parts, _, depth = runs[0].shape
    tokens = sum(run.shape[1] for run in runs)
    width = weights.shape[-1]
    return pl.pallas_call(
        project_kernel,
        grid_spec=pltpu.PrefetchScalarGridSpec(
            num_scalar_prefetch=1,
            grid=(2,),
            in_specs=[pl.BlockSpec(run.shape, lambda s, side: (0, 0, 0)) for run in runs]
            + [pl.BlockSpec((1, parts, 1, depth, width), lambda s, side: (side[0], 0, s, 0, 0))],
            out_specs=pl.BlockSpec((1, tokens, width), lambda s, side: (s, 0, 0)),
        ),
        out_shape=jax.ShapeDtypeStruct((2, tokens, width), BF16),
        compiler_params=pltpu.CompilerParams(vmem_limit_bytes=48 * 1024 * 1024),
        name="project",
    )(jnp.reshape(side, (1,)).astype(jnp.int32), *runs, weights)


def swapped_pairs():
    pairs = []
    for ctx in range(16):
        for chan in range(16):
            inner, ring = (ctx >> 1) & 3, (chan >> 1) & 3
            to_ctx = (ctx & 9) | (ring << 1)
            to_chan = (chan & 9) | (inner << 1)
            pairs.append((ctx * 16 + chan, to_ctx * 16 + to_chan))
    return pairs


def grouped(value, groups):
    return lax.all_to_all(
        value, "chan", split_axis=0, concat_axis=0, tiled=True, axis_index_groups=groups
    )


def pool_pieces(pool_tails):
    pool_dev, sets, tail, channels = pool_tails.shape
    rows = jnp.transpose(pool_tails, (1, 2, 0, 3)).reshape(sets * tail, pool_dev, channels)
    count = lax.axis_size("ctx")
    each = -(-(sets * tail) // count)
    rows = jnp.pad(rows, ((0, each * count - sets * tail), (0, 0), (0, 0)))
    return rows.reshape(count, each, pool_dev, channels)


def chosen_pieces(pieces, stripe_request, hit_holder, hit_block):
    count, _, pool_dev, _ = pieces.shape
    request = jnp.arange(hit_holder.shape[0], dtype=jnp.int32)
    ours = (stripe_request[:, None] == request[None, :]).astype(jnp.int32)
    holder = jnp.sum(ours * hit_holder[None, :], axis=1)
    block = jnp.sum(ours * hit_block[None, :], axis=1)
    select = jnp.logical_and(
        holder[:, None, None] == jnp.arange(count, dtype=jnp.int32)[None, :, None],
        block[:, None, None] == jnp.arange(pool_dev, dtype=jnp.int32)[None, None, :],
    ).astype(BF16)
    return jnp.einsum("dhb,hrbc->drc", select, pieces, preferred_element_type=F32).astype(BF16)


def exchanged(value):
    return lax.all_to_all(value, "ctx", split_axis=0, concat_axis=0, tiled=True)


def body(
    features,
    pool_tails,
    short_filter,
    long_filter,
    skip_gain,
    out_weight,
    stripe_request,
    hit_holder,
    hit_block,
):
    sets, tokens, channels = features.shape
    tail = pool_tails.shape[2]
    split = 2 * LANES
    my_index = lax.axis_index("ctx")
    rings = [[j | (r << 1) for r in range(4)] for j in (0, 1, 8, 9)]

    def spread(gated):
        return grouped(jnp.broadcast_to(gated, (4, *gated.shape)), rings)

    swapped = lax.ppermute(out_weight, ("ctx", "chan"), swapped_pairs())
    taps = jnp.transpose(short_filter, (1, 0, 2)).astype(F32)
    skip = skip_gain[None, :]
    band = toeplitz(long_filter)
    pieces, band = lax.optimization_barrier((pool_pieces(pool_tails), band))
    pieces = exchanged(pieces)
    late = gated_tokens(
        features[:, split - HEAD : split, :], features[:, split:, :], taps, skip, band
    )
    previous = lax.ppermute(
        features[:, tokens - HEAD :, :], "ctx", [(i, i + 1) for i in range(15)]
    )
    pulled = exchanged(chosen_pieces(pieces, stripe_request, hit_holder, hit_block))
    swapped, pulled, late = lax.optimization_barrier((swapped, pulled, late))
    weights = lax.all_gather(swapped, "ctx", axis=0, tiled=True)
    weights = weights.reshape(2, 4, 2, *out_weight.shape)
    late = spread(late)
    pulled = pulled.reshape(-1, channels)[: sets * tail].reshape(sets, tail, channels)

    order = jnp.arange(stripe_request.shape[0], dtype=jnp.int32)
    request = jnp.sum(jnp.where(order == my_index, stripe_request, 0))
    earlier = jnp.sum(jnp.where(order == my_index - 1, stripe_request, 0))
    starting = jnp.logical_or(my_index == 0, earlier != request)
    pulled = jnp.pad(pulled, ((0, 0), (HEAD - tail, 0), (0, 0)))
    head = jnp.where(starting, pulled, previous)
    early = gated_tokens(head, features[:, :split, :], taps, skip, band)
    early, late = lax.optimization_barrier((early, late))
    early, late = [spread(early)], [late]

    chan = lax.axis_index("chan")
    high, low = chan >> 3, chan & 1

    def flipped(value, bit):
        return lax.ppermute(value, "chan", [(j, j ^ bit) for j in range(16)])

    def halves(kept, came):
        kept = kept.astype(F32) + came.astype(F32)
        mine = jnp.where(low == 0, kept[0], kept[1])
        other = jnp.where(low == 0, kept[1], kept[0])
        return mine, other.astype(BF16)

    def rounded(mine, came):
        return (mine + came.astype(F32)).astype(BF16)

    late_came = flipped(project(late, weights, 1 - high), 8)
    late_kept = project(late, weights, high)
    early, late_kept = lax.optimization_barrier((early, late_kept))
    early_came = flipped(project(early, weights, 1 - high), 8)
    late_mine, late_other = halves(late_kept, late_came)
    early, late_other = lax.optimization_barrier((early, late_other))
    late_came = flipped(late_other, 1)
    early_mine, early_other = halves(project(early, weights, high), early_came)
    early_came = flipped(early_other, 1)
    return jnp.concatenate(
        [rounded(early_mine, early_came), rounded(late_mine, late_came)], axis=0
    )


def solution(mesh):
    return jax.shard_map(
        body,
        mesh=mesh,
        in_specs=(
            P(None, "ctx", "chan"),
            P("ctx", None, None, "chan"),
            P(None, None, "chan"),
            P("chan", None),
            P("chan"),
            P("chan", "ctx"),
            P(),
            P(),
            P(),
        ),
        out_specs=P("ctx", "chan"),
        check_vma=False,
    )
```
